32 devices in a mesh: group: 2 (over y), expert: 16 (over z, x, core), tensor: 1.
Axes of the slice: x: 2, y: 2, z: 4, core: 2. Of those that a mesh axis runs over, the one named last changes fastest.
Arguments:
- residual: bfloat16 [2048, 3584], P(('group', 'expert'), 'tensor'), parts along dimension 0, may hold values from -6 to 6
- attn_partial: bfloat16 [1, 2048, 3584], P('tensor', ('group', 'expert')), parts along dimension 1, may hold values from -6 to 6
- norm_gain: float32 [3584], replicated, may hold values from 0.25 to 1.75
- router_weight: bfloat16 [3584, 16], P('tensor'), may hold values from -0.1875 to 0.1875
- expert_ids: int32 [2048, 8], P(('group', 'expert')), parts along dimension 0, may hold values from 0 to 15, all different within a row; in each aligned block of 64 rows (0 to 63, 64 to 127, ...) at most 56 rows name the same one
- expert_weight: bfloat16 [16, 3584, 1024], P('expert', None, 'tensor'), may hold values from -0.1875 to 0.1875
Outputs:
- layer_out: bfloat16 [2048, 3584], P(('group', 'expert'), 'tensor'), parts along dimension 0
The draws below stay inside these ranges and needn't reach their ends.
There are 2 independent parts, one for each index of `group`. The reference program is written for one: setup_inputs(seed, part) draws one part's arguments, and reference() takes and returns one part's arrays. A program takes and returns all parts, laid end to end along the dimension named above; an argument that names none is the same for every part. Nothing has to cross between parts.
Inputs may be any that keep to these rules, and one draw needn't show every extreme that they name: `expert_ids`: the 8 experts of a row are distinct. Among the rows of one device (aligned blocks of 64 rows) no expert is named more than 56 times, a bound that some block reaches.
All inputs are finite; a program needn't handle non-finite values.
Results may differ from the reference program's by a relative error of at most 0.015.
Values may be sent and summed in bfloat16 or wider, within the bound.
A program may use at most 64 MiB of HBM per device.

```python
import math
import jax
import jax.numpy as jnp
import numpy as np
from jax import lax

D = 3584
FF = 1024
TOPK = 8
QBLOCK = 128
ROW_DEV = 64
EXPERTS = 16
ROWS = 1024
CAP = 56
TP_PARTS = 1
N_EXPERT = 16


def steps_of(stream_key, extent, cuts, low, top_value):
    gain = 1.0
    for dim, shards_of in cuts:
        draws = jax.random.uniform(jax.random.fold_in(jax.random.fold_in(stream_key, 6), dim), (shards_of,), jnp.float32, low / len(cuts), top_value / len(cuts))
        gain = gain * jnp.repeat(jnp.exp(draws), extent[dim] // shards_of).reshape((-1,) + (1,) * (len(extent) - 1 - dim))
    return gain


def assign_block(rng, own, number, rows, number_of, top, most, skew):
    order = jax.random.permutation(rng, number_of)
    crowded, common = load_shares(number_of, rows * top, most, skew, True), load_shares(number_of, rows * top, most, skew, False)
    places = jnp.arange(number_of)

    def named(sizes, offset_by):
        used = int((sizes > 0).sum())
        fixed = max(1, used // 4)
        moved = fixed + (places - fixed + offset_by * (used - fixed)) % max(1, number_of - fixed)
        return jnp.zeros((number_of,), jnp.int32).at[order[jnp.where(places < fixed, places, moved)]].set(jnp.asarray(sizes, jnp.int32))

    sizes = jnp.where(number % 4 == 0, named(crowded, number // 4), named(common, number - number // 4 - 1))
    mixed = jax.random.permutation(jax.random.fold_in(own, 3), number_of)
    giver, receiver = mixed[0:number_of // 2 * 2:2], mixed[1:number_of // 2 * 2:2]
    room = jnp.minimum(sizes[giver] - 1, most - sizes[receiver]) // 2
    room = jnp.where((giver == order[0]) | (receiver == order[0]) | (sizes[receiver] == 0), 0, jnp.maximum(room, 0))
    moved = jax.random.randint(jax.random.fold_in(own, 4), (number_of // 2,), 0, 1 << 20) % (room + 1)
    sizes = sizes.at[giver].add(-moved).at[receiver].add(moved)
    labels = jnp.searchsorted(jnp.cumsum(sizes), jnp.arange(rows * top), side="right").astype(jnp.int32)
    grid = labels.reshape(top, rows).T
    grid = grid[jax.random.permutation(jax.random.fold_in(own, 1), rows)]
    offset_by = jax.random.randint(jax.random.fold_in(own, 2), (rows, 1), 0, top)
    return jnp.take_along_axis(grid, (jnp.arange(top)[None, :] + offset_by) % top, axis=1)


def load_shares(amount, total, most, lean, full):
    weights = [(1 << 20) // math.isqrt(standing ** lean) + 1 for standing in range(1, amount + 1)]
    largest = most if full else min(most, max(-(-total // amount), total * weights[0] // sum(weights)))
    least = 1 if total - largest >= amount - 1 else 0
    counts, rest = [largest] + [least] * (amount - 1), total - largest - least * (amount - 1)
    while rest > 0:
        free = [i for i in range(1, amount) if counts[i] < largest] or [i for i in range(1, amount) if counts[i] < most]
        mass, remaining = sum([weights[i] for i in free]), rest
        for i in free:
            more = min(most - counts[i], max(1, remaining * weights[i] // mass), rest)
            counts[i] = counts[i] + more
            rest = rest - more
    return np.array(counts)


def bell_draw(rng, dims, deviation, bound, shards=(), kind=jnp.bfloat16):
    values = deviation * jax.random.normal(rng, dims, jnp.float32)
    if shards:
        values = values * steps_of(rng, dims, shards, -0.22, 0.18)
    return jnp.clip(values, -bound, bound).astype(kind)


def setup_inputs(seed: int = 0, part: int = 0) -> dict:
    keys = jax.random.split(jax.random.key(seed), 7)
    own_keys = jax.random.split(jax.random.fold_in(keys[6], part), 7)
    residual = bell_draw(own_keys[0], (ROWS, D), 1.0, 6.0, ((0, 16),))
    attn_partial = bell_draw(own_keys[1], (TP_PARTS, ROWS, D), 1.0, 6.0, ((1, 16),))
    norm_gain = jnp.clip(1.0 + 0.15 * jax.random.normal(keys[2], (D,), jnp.float32), 0.25, 1.75)
    router_weight = bell_draw(keys[3], (D, EXPERTS), (D // 4) ** -0.5, 0.1875)
    expert_ids_keys = jax.random.split(jax.random.fold_in(own_keys[4], 1), ROWS // ROW_DEV)
    expert_ids_turns = jax.random.permutation(jax.random.fold_in(own_keys[4], 3), ROWS // ROW_DEV)
    expert_ids = jax.vmap(lambda own, number: assign_block(jax.random.fold_in(own_keys[4], 2), own, number, ROW_DEV, EXPERTS, TOPK, CAP, 2))(expert_ids_keys, expert_ids_turns).reshape((ROWS, TOPK))
    expert_weight = bell_draw(keys[5], (EXPERTS, D, FF), (D // 4) ** -0.5, 0.1875, ((0, 16),))
    return {"residual": residual, "attn_partial": attn_partial, "norm_gain": norm_gain, "router_weight": router_weight, "expert_ids": expert_ids, "expert_weight": expert_weight}


EPS = 1e-06
ROUTE_SCALE = 2.5

def restore_rows(values):
    row_count, columns = values.shape
    blocks = values.astype(jnp.float32).reshape(row_count, columns // QBLOCK, QBLOCK)
    largest = lax.optimization_barrier(jnp.max(jnp.abs(blocks), axis=-1))
    block_scale = ((largest + EPS) / 448.0).astype(jnp.bfloat16)
    encoded = (blocks / block_scale.astype(jnp.float32)[:, :, None]).astype(jnp.bfloat16)
    restored = (encoded.astype(jnp.float32) * block_scale.astype(jnp.float32)[:, :, None]).astype(jnp.bfloat16)
    return restored.reshape(row_count, columns)

def block_slots(block_ids):
    onehot = (block_ids[:, None] == jnp.arange(EXPERTS, dtype=jnp.int32)[None, :]).astype(jnp.int32)
    before = jnp.cumsum(onehot, axis=0) - onehot
    return lax.optimization_barrier(jnp.sum(before * onehot, axis=1)).astype(jnp.int32)

def reference(residual, attn_partial, norm_gain, router_weight, expert_ids, expert_weight):
    stream = residual.astype(jnp.float32) + lax.optimization_barrier(jnp.sum(attn_partial.astype(jnp.float32), axis=0))
    meansq = lax.optimization_barrier(jnp.mean(stream * stream, axis=1, keepdims=True))
    normed = (stream * lax.rsqrt(meansq + EPS) * norm_gain).astype(jnp.bfloat16)
    logits = jnp.dot(normed, router_weight, preferred_element_type=jnp.float32)
    affinity = jax.nn.sigmoid(logits)
    chosen = expert_ids[:, :, None] == jnp.arange(EXPERTS, dtype=jnp.int32)[None, None, :]
    picked = lax.optimization_barrier(jnp.sum(jnp.where(chosen, affinity[:, None, :], 0.0), axis=2))
    gate_values = ROUTE_SCALE * picked / lax.optimization_barrier(jnp.sum(picked, axis=1, keepdims=True))
    restored = restore_rows(normed)
    flat_ids = expert_ids.reshape(-1).astype(jnp.int32)
    slot_index = lax.map(block_slots, flat_ids.reshape(N_EXPERT, ROW_DEV * TOPK)).reshape(-1)
    pick_index = jnp.arange(ROWS * TOPK, dtype=jnp.int32)
    position = pick_index // (ROW_DEV * TOPK) * CAP + slot_index
    row_table = jnp.zeros((EXPERTS, N_EXPERT * CAP), jnp.int32).at[flat_ids, position].set(pick_index // TOPK)
    gate_table = jnp.zeros((EXPERTS, N_EXPERT * CAP), jnp.float32).at[flat_ids, position].set(gate_values.reshape(-1))
    half_units = FF // TP_PARTS

    def add_expert(total, inputs):
        rows_here, gates_here, w_expert = inputs
        taken = restored[rows_here]
        hidden = jax.nn.silu(jnp.dot(taken, w_expert, preferred_element_type=jnp.float32)).astype(jnp.bfloat16)
        output = jnp.zeros((rows_here.shape[0], D), jnp.float32)
        for part_index in range(TP_PARTS):
            lower = part_index * half_units
            piece = lax.dot_general(hidden[:, lower:lower + half_units], w_expert[:, lower:lower + half_units], (((1,), (1,)), ((), ())), preferred_element_type=jnp.float32).astype(jnp.bfloat16)
            output = output + piece.astype(jnp.float32)
        rounded = lax.optimization_barrier(output.astype(jnp.bfloat16))
        return (total.at[rows_here].add(gates_here[:, None] * rounded.astype(jnp.float32)), None)
    moe, _ = lax.scan(add_expert, jnp.zeros((ROWS, D), jnp.float32), (row_table, gate_table, expert_weight))
    return (stream + moe).astype(jnp.bfloat16)
```

```python
import jax
import jax.numpy as jnp
from jax import lax
from jax.sharding import PartitionSpec as P

QBLOCK = 128


EPS = 1e-06
ROUTE_SCALE = 2.5


def encode(values):
    row_count, columns = values.shape
    blocks = values.astype(jnp.float32).reshape(row_count, columns // QBLOCK, QBLOCK)
    largest = jnp.max(jnp.abs(blocks), axis=-1)
    block_scale = ((largest + EPS) / 448.0).astype(jnp.bfloat16)
    encoded = (blocks / block_scale.astype(jnp.float32)[:, :, None]).astype(jnp.bfloat16)
    return (encoded.reshape(row_count, columns), block_scale)


def decode(encoded, block_scale):
    leading = encoded.shape[:-1]
    columns = encoded.shape[-1]
    blocks = encoded.astype(jnp.float32).reshape(leading + (columns // QBLOCK, QBLOCK))
    restored = (blocks * block_scale.astype(jnp.float32)[..., None]).astype(jnp.bfloat16)
    return restored.reshape(leading + (columns,))


def local(residual, attn_partial, norm_gain, router_weight, expert_ids, expert_weight):
    row_count, share_width = residual.shape
    tensor_count = lax.axis_size("tensor")
    model_width = share_width * tensor_count
    expert_count = router_weight.shape[1]
    top_count = expert_ids.shape[1]
    capacity = min(row_count, max(2, 7 * row_count * top_count // (4 * expert_count)))
    first_column = lax.axis_index("tensor") * share_width
    partial_attn = attn_partial[0].astype(jnp.float32)
    full_residual = lax.all_gather(residual, "tensor", axis=1, tiled=True)
    attention = lax.psum(partial_attn.astype(jnp.bfloat16), "tensor").astype(jnp.float32)
    stream = full_residual.astype(jnp.float32) + attention
    meansq = jnp.mean(stream * stream, axis=1, keepdims=True)
    normed = (stream * lax.rsqrt(meansq + EPS) * norm_gain).astype(jnp.bfloat16)
    normed_share = lax.dynamic_slice_in_dim(normed, first_column, share_width, 1)
    stream_share = lax.dynamic_slice_in_dim(stream, first_column, share_width, 1)
    logits = lax.psum(
        jnp.dot(normed_share, router_weight, preferred_element_type=jnp.float32).astype(
            jnp.bfloat16
        ),
        "tensor",
    ).astype(jnp.float32)
    affinity = jax.nn.sigmoid(logits)
    chosen = expert_ids[:, :, None] == jnp.arange(expert_count, dtype=jnp.int32)[None, None, :]
    picked = jnp.sum(jnp.where(chosen, affinity[:, None, :], 0.0), axis=2)
    gate_values = ROUTE_SCALE * picked / jnp.sum(picked, axis=1, keepdims=True)
    encoded, block_scale = encode(normed)
    flat_ids = expert_ids.reshape(-1)
    onehot = (flat_ids[:, None] == jnp.arange(expert_count, dtype=jnp.int32)[None, :]).astype(
        jnp.int32
    )
    before = jnp.cumsum(onehot, axis=0) - onehot
    slot_index = jnp.sum(before * onehot, axis=1)
    target_slot = flat_ids * capacity + slot_index
    source_row = jnp.arange(row_count * top_count, dtype=jnp.int32) // top_count
    send_codes = (
        jnp.zeros((expert_count * capacity, encoded.shape[1]), jnp.bfloat16)
        .at[target_slot]
        .set(encoded[source_row])
    )
    send_scales = (
        jnp.zeros((expert_count * capacity, block_scale.shape[1]), jnp.bfloat16)
        .at[target_slot]
        .set(block_scale[source_row])
    )
    send_codes = send_codes.reshape(expert_count, 1, capacity, encoded.shape[1])
    send_scales = send_scales.reshape(expert_count, 1, capacity, block_scale.shape[1])
    codes_in = lax.all_to_all(send_codes, "expert", split_axis=0, concat_axis=1, tiled=True)
    scales_in = lax.all_to_all(send_scales, "expert", split_axis=0, concat_axis=1, tiled=True)
    inputs = decode(codes_in, scales_in)
    leading = inputs.shape[:-1]
    flat_rows = inputs.reshape(-1, model_width)
    w_expert = expert_weight[0]
    hidden = jax.nn.silu(jnp.dot(flat_rows, w_expert, preferred_element_type=jnp.float32)).astype(
        jnp.bfloat16
    )
    output = lax.dot_general(
        hidden, w_expert, (((1,), (1,)), ((), ())), preferred_element_type=jnp.float32
    ).astype(jnp.bfloat16)
    halves = output.reshape(leading + (tensor_count, 1, share_width))
    returned = lax.all_to_all(
        lax.all_to_all(halves, "expert", split_axis=1, concat_axis=0, tiled=True),
        "tensor",
        split_axis=3,
        concat_axis=4,
        tiled=True,
    )
    expert_out = jnp.sum(returned.astype(jnp.float32), axis=(3, 4)).astype(jnp.bfloat16)
    taken = expert_out.reshape(expert_count * capacity, share_width)[target_slot]
    taken = taken.reshape(row_count, top_count, share_width)
    moe_share = jnp.einsum("rk,rkd->rd", gate_values, taken.astype(jnp.float32))
    return (stream_share + moe_share).astype(jnp.bfloat16)


def local_rows(residual, attn_partial, norm_gain, router_weight, expert_ids):
    expert_count = router_weight.shape[1]
    stream = residual.astype(jnp.float32) + attn_partial[0].astype(jnp.float32)
    meansq = jnp.mean(stream * stream, axis=1, keepdims=True)
    normed = (stream * lax.rsqrt(meansq + EPS) * norm_gain).astype(jnp.bfloat16)
    logits = jnp.dot(normed, router_weight, preferred_element_type=jnp.float32)
    affinity = jax.nn.sigmoid(logits)
    chosen = expert_ids[:, :, None] == jnp.arange(expert_count, dtype=jnp.int32)[None, None, :]
    picked = jnp.where(jnp.any(chosen, axis=1), affinity, 0.0)
    gates = ROUTE_SCALE * picked / jnp.sum(picked, axis=1, keepdims=True)
    encoded, block_scale = encode(normed)
    restored = decode(encoded, block_scale)
    return stream, gates, restored


def local_dense(residual, attn_partial, norm_gain, router_weight, expert_ids, expert_weight):
    stream, gates, restored = local_rows(
        residual, attn_partial, norm_gain, router_weight, expert_ids
    )
    rows = lax.all_gather(restored, "expert", axis=0, tiled=True)
    all_gates = lax.all_gather(gates, "expert", axis=0, tiled=True)
    gate = lax.dynamic_slice_in_dim(all_gates, lax.axis_index("expert"), 1, 1)
    w_expert = expert_weight[0]
    hidden = jax.nn.silu(jnp.dot(rows, w_expert, preferred_element_type=jnp.float32)).astype(
        jnp.bfloat16
    )
    output = lax.dot_general(
        hidden, w_expert, (((1,), (1,)), ((), ())), preferred_element_type=jnp.float32
    ).astype(jnp.bfloat16)
    share = (output.astype(jnp.float32) * gate).astype(jnp.bfloat16)
    moe = lax.psum_scatter(share, "expert", scatter_dimension=0, tiled=True)
    return (stream + moe.astype(jnp.float32)).astype(jnp.bfloat16)


def dense_fits(mesh, row_count, expert_count, top_count):
    return (
        mesh.shape["tensor"] == 1
        and mesh.shape["expert"] == expert_count
        and expert_count <= 4 * top_count
    )


def solution(mesh):
    placed = (
        P(("group", "expert"), "tensor"),
        P("tensor", ("group", "expert"), None),
        P(),
        P("tensor", None),
        P(("group", "expert"), None),
        P("expert", None, "tensor"),
    )

    def run(residual, attn_partial, norm_gain, router_weight, expert_ids, expert_weight):
        dense = dense_fits(mesh, residual.shape[0], router_weight.shape[1], expert_ids.shape[1])
        return jax.shard_map(
            local_dense if dense else local,
            mesh=mesh,
            in_specs=placed,
            out_specs=P(("group", "expert"), "tensor"),
            check_vma=False,
        )(residual, attn_partial, norm_gain, router_weight, expert_ids, expert_weight)

    return run
```

```python
import jax
import jax.numpy as jnp
from jax import lax
from jax.experimental import pallas as pl
from jax.experimental.pallas import tpu as pltpu
from jax.sharding import PartitionSpec as P

QBLOCK = 128


EPS = 1e-06
ROUTE_SCALE = 2.5


def encode(values):
    row_count, columns = values.shape
    blocks = values.astype(jnp.float32).reshape(row_count, columns // QBLOCK, QBLOCK)
    largest = jnp.max(jnp.abs(blocks), axis=-1)
    block_scale = ((largest + EPS) / 448.0).astype(jnp.bfloat16)
    encoded = (blocks / block_scale.astype(jnp.float32)[:, :, None]).astype(jnp.bfloat16)
    return (encoded.reshape(row_count, columns), block_scale)


def decode(encoded, block_scale):
    leading = encoded.shape[:-1]
    columns = encoded.shape[-1]
    blocks = encoded.astype(jnp.float32).reshape(leading + (columns // QBLOCK, QBLOCK))
    restored = (blocks * block_scale.astype(jnp.float32)[..., None]).astype(jnp.bfloat16)
    return restored.reshape(leading + (columns,))


def local(residual, attn_partial, norm_gain, router_weight, expert_ids, expert_weight):
    row_count, share_width = residual.shape
    tensor_count = lax.axis_size("tensor")
    model_width = share_width * tensor_count
    expert_count = router_weight.shape[1]
    top_count = expert_ids.shape[1]
    capacity = min(row_count, max(2, 7 * row_count * top_count // (4 * expert_count)))
    first_column = lax.axis_index("tensor") * share_width
    partial_attn = attn_partial[0].astype(jnp.float32)
    full_residual = lax.all_gather(residual, "tensor", axis=1, tiled=True)
    attention = lax.psum(partial_attn.astype(jnp.bfloat16), "tensor").astype(jnp.float32)
    stream = full_residual.astype(jnp.float32) + attention
    meansq = jnp.mean(stream * stream, axis=1, keepdims=True)
    normed = (stream * lax.rsqrt(meansq + EPS) * norm_gain).astype(jnp.bfloat16)
    normed_share = lax.dynamic_slice_in_dim(normed, first_column, share_width, 1)
    stream_share = lax.dynamic_slice_in_dim(stream, first_column, share_width, 1)
    logits = lax.psum(
        jnp.dot(normed_share, router_weight, preferred_element_type=jnp.float32).astype(
            jnp.bfloat16
        ),
        "tensor",
    ).astype(jnp.float32)
    affinity = jax.nn.sigmoid(logits)
    chosen = expert_ids[:, :, None] == jnp.arange(expert_count, dtype=jnp.int32)[None, None, :]
    picked = jnp.sum(jnp.where(chosen, affinity[:, None, :], 0.0), axis=2)
    gate_values = ROUTE_SCALE * picked / jnp.sum(picked, axis=1, keepdims=True)
    encoded, block_scale = encode(normed)
    flat_ids = expert_ids.reshape(-1)
    onehot = (flat_ids[:, None] == jnp.arange(expert_count, dtype=jnp.int32)[None, :]).astype(
        jnp.int32
    )
    before = jnp.cumsum(onehot, axis=0) - onehot
    slot_index = jnp.sum(before * onehot, axis=1)
    target_slot = flat_ids * capacity + slot_index
    source_row = jnp.arange(row_count * top_count, dtype=jnp.int32) // top_count
    send_codes = (
        jnp.zeros((expert_count * capacity, encoded.shape[1]), jnp.bfloat16)
        .at[target_slot]
        .set(encoded[source_row])
    )
    send_scales = (
        jnp.zeros((expert_count * capacity, block_scale.shape[1]), jnp.bfloat16)
        .at[target_slot]
        .set(block_scale[source_row])
    )
    send_codes = send_codes.reshape(expert_count, 1, capacity, encoded.shape[1])
    send_scales = send_scales.reshape(expert_count, 1, capacity, block_scale.shape[1])
    codes_in = lax.all_to_all(send_codes, "expert", split_axis=0, concat_axis=1, tiled=True)
    scales_in = lax.all_to_all(send_scales, "expert", split_axis=0, concat_axis=1, tiled=True)
    inputs = decode(codes_in, scales_in)
    leading = inputs.shape[:-1]
    flat_rows = inputs.reshape(-1, model_width)
    w_expert = expert_weight[0]
    hidden = jax.nn.silu(jnp.dot(flat_rows, w_expert, preferred_element_type=jnp.float32)).astype(
        jnp.bfloat16
    )
    output = lax.dot_general(
        hidden, w_expert, (((1,), (1,)), ((), ())), preferred_element_type=jnp.float32
    ).astype(jnp.bfloat16)
    halves = output.reshape(leading + (tensor_count, 1, share_width))
    returned = lax.all_to_all(
        lax.all_to_all(halves, "expert", split_axis=1, concat_axis=0, tiled=True),
        "tensor",
        split_axis=3,
        concat_axis=4,
        tiled=True,
    )
    expert_out = jnp.sum(returned.astype(jnp.float32), axis=(3, 4)).astype(jnp.bfloat16)
    taken = expert_out.reshape(expert_count * capacity, share_width)[target_slot]
    taken = taken.reshape(row_count, top_count, share_width)
    moe_share = jnp.einsum("rk,rkd->rd", gate_values, taken.astype(jnp.float32))
    return (stream_share + moe_share).astype(jnp.bfloat16)


def local_rows(residual, attn_partial, norm_gain, router_weight, expert_ids):
    expert_count = router_weight.shape[1]
    stream = residual.astype(jnp.float32) + attn_partial[0].astype(jnp.float32)
    meansq = jnp.mean(stream * stream, axis=1, keepdims=True)
    normed = (stream * lax.rsqrt(meansq + EPS) * norm_gain).astype(jnp.bfloat16)
    logits = jnp.dot(normed, router_weight, preferred_element_type=jnp.float32)
    affinity = jax.nn.sigmoid(logits)
    chosen = expert_ids[:, :, None] == jnp.arange(expert_count, dtype=jnp.int32)[None, None, :]
    picked = jnp.where(jnp.any(chosen, axis=1), affinity, 0.0)
    gates = ROUTE_SCALE * picked / jnp.sum(picked, axis=1, keepdims=True)
    encoded, block_scale = encode(normed)
    restored = decode(encoded, block_scale)
    return stream, gates, restored


def moe_kernel(own_ref, stream_in, weight_hbm, out_ref, rows, weight, stream_ref, share, hidden, core_in, x_in,
               chain_in, weight_sem, put_sem, line_send, x_send, core_send, row_recv,
               pair_send, pair_recv, half_send, half_recv, chain_send, chain_recv):
    block_rows, width = out_ref.shape
    tile = 256
    me = lax.axis_index("expert")
    z, x, c = me // 4, (me // 2) % 2, me % 2
    flip = z // 2
    m = z + flip * (3 - 2 * z)

    def expert_at(zz, xx, cc):
        return (zz * 2 + xx) * 2 + cc

    def place(o):
        return o + flip * (3 - 2 * o)

    def to(zz, xx, cc):
        return {"expert": expert_at(zz, xx, cc)}

    def slot(zz, xx, cc):
        return rows.at[zz, pl.ds(pl.multiple_of(block_rows * (2 * xx + cc), block_rows), block_rows), :]

    barrier = pltpu.get_barrier_semaphore()

    def greet(device):
        pl.semaphore_signal(barrier, inc=1, device_id=device, device_id_type=pl.DeviceIdType.MESH)

    load_weight = pltpu.make_async_copy(weight_hbm.at[0], weight, weight_sem)
    load_weight.start()
    put_own = pltpu.make_async_copy(own_ref, slot(z, x, c), put_sem)
    put_own.start()
    greet(to(z, 1 - x, c))
    greet(to(z, x, 1 - c))
    pl.when(z > 0)(lambda: greet(to(z - 1, x, c)))
    pl.when(z < 3)(lambda: greet(to(z + 1, x, c)))
    put_own.wait()
    pl.semaphore_wait(barrier, 3 + m)

    def row_copy(zz, xx, cc, sem, device):
        part = slot(zz, xx, cc)
        return pltpu.make_async_remote_copy(
            src_ref=part, dst_ref=part, send_sem=sem, recv_sem=row_recv.at[expert_at(zz, xx, cc)],
            device_id=device, device_id_type=pl.DeviceIdType.MESH,
        )

    def up_copy(p):
        return row_copy(p, x, c, line_send.at[0, p], to(z + 1, x, c))

    def down_copy(p):
        return row_copy(p, x, c, line_send.at[1, p], to(z - 1, x, c))

    def x_copy(p):
        return row_copy(p, x, c, x_send.at[p], to(z, 1 - x, c))

    def core_copy(p, xx):
        return row_copy(p, xx, c, core_send.at[p, xx], to(z, x, 1 - c))

    def got(zz, xx, cc):
        row_copy(zz, xx, cc, x_send.at[0], to(z, 1 - x, c)).wait_recv()

    def pass_on(p):
        pl.when((p <= z) & (z < 3))(lambda: up_copy(p).start())
        pl.when((p >= z) & (z > 0))(lambda: down_copy(p).start())
        x_copy(p).start()
        core_copy(p, x).start()

    def arrive_line(p):
        got(p, x, c)
        pass_on(p)

    def pair_copy(p):
        return pltpu.make_async_remote_copy(
            src_ref=share.at[p, 1 - c], dst_ref=core_in.at[p],
            send_sem=pair_send.at[p], recv_sem=pair_recv.at[p],
            device_id=to(z, x, 1 - c), device_id_type=pl.DeviceIdType.MESH,
        )

    def half_copy(p):
        return pltpu.make_async_remote_copy(
            src_ref=share.at[p, c, 1 - x], dst_ref=x_in.at[p],
            send_sem=half_send.at[p], recv_sem=half_recv.at[p],
            device_id=to(z, 1 - x, c), device_id_type=pl.DeviceIdType.MESH,
        )

    def chain_copy(p, towards, index):
        return pltpu.make_async_remote_copy(
            src_ref=share.at[p, c, x], dst_ref=chain_in.at[index],
            send_sem=chain_send.at[p], recv_sem=chain_recv.at[index],
            device_id=to(towards, x, c), device_id_type=pl.DeviceIdType.MESH,
        )

    def send_chain(p, act):
        pl.when(p > z)(lambda: act(chain_copy(p, z + 1, p)))
        pl.when(p == z - 1)(lambda: act(chain_copy(p, z - 1, 4)))
        pl.when(p < z - 1)(lambda: act(chain_copy(p, z - 1, p)))

    def compute(p):
        units = weight.shape[1]
        gate_block = rows[p, :, width:].astype(jnp.float32)
        lane = lax.broadcasted_iota(jnp.int32, gate_block.shape, 1)
        mine = (lane == me) | (lane == me + 64)
        gate = jnp.sum(jnp.where(mine, gate_block, 0.0), axis=1, keepdims=True)

        def first(n, carry):
            columns = pl.ds(pl.multiple_of(n * tile, tile), tile)
            v = jnp.dot(rows[p, :, :width], weight[:, columns], preferred_element_type=jnp.float32)
            hidden[:, columns] = (v / (1.0 + jnp.exp(-v))).astype(jnp.bfloat16)
            return carry

        lax.fori_loop(0, units // tile, first, 0)

        def second(n, carry):
            columns = pl.ds(pl.multiple_of(n * tile, tile), tile)
            v = lax.dot_general(
                hidden[...], weight[columns, :], (((1,), (1,)), ((), ())),
                preferred_element_type=jnp.float32,
            )
            v = v.astype(jnp.bfloat16).astype(jnp.float32) * gate
            v = v.astype(jnp.bfloat16)
            for i in range(4):
                share[p, i % 2, i // 2, :, columns] = v[i * block_rows:(i + 1) * block_rows]
            return carry

        lax.fori_loop(0, width // tile, second, 0)

    def add_pair(p):
        pair_copy(p).wait_recv()
        for xx in range(2):
            share[p, c, xx] = (
                share[p, c, xx].astype(jnp.float32) + core_in[p, xx].astype(jnp.float32)
            ).astype(jnp.bfloat16)
        half_copy(p).start()

    def add_half(p):
        half_copy(p).wait_recv()
        has = ((p > z) & (z > 0)) | ((p < z) & (z < 3))

        @pl.when(has)
        def _():
            chain_copy(p, z, p).wait_recv()
            share[p, c, x] = (
                share[p, c, x].astype(jnp.float32) + x_in[p].astype(jnp.float32)
                + chain_in[p].astype(jnp.float32)
            ).astype(jnp.bfloat16)

        @pl.when(jnp.logical_not(has))
        def _():
            share[p, c, x] = (
                share[p, c, x].astype(jnp.float32) + x_in[p].astype(jnp.float32)
            ).astype(jnp.bfloat16)

        send_chain(p, lambda copy: copy.start())

    pass_on(z)
    middle = m == 1

    def step(k, carry):
        own_order = jnp.where(k == 0, m, jnp.where(k == 1, 1 - m, k))
        p = place(own_order)
        later = place(jnp.where(k == 0, 1 - m, k + 1))
        pl.when(k < 3 - 2 * m)(lambda: arrive_line(later))
        pl.when(middle & (k == 0))(lambda: arrive_line(place(2)))
        pl.when(middle & (k == 1))(lambda: arrive_line(place(3)))
        got(p, 1 - x, c)
        core_copy(p, 1 - x).start()
        pl.when(k == 3)(lambda: add_pair(place(2)))
        got(p, x, 1 - c)
        got(p, 1 - x, 1 - c)
        pl.when(k == 0)(lambda: load_weight.wait())
        compute(p)
        pair_copy(p).start()
        return carry

    lax.fori_loop(0, 4, step, 0)

    order = [place(2), place(3), place(1 - m), z]
    add_pair(order[1])
    add_half(order[0])
    add_pair(order[2])
    add_half(order[1])
    add_pair(order[3])
    add_half(order[2])
    half_copy(z).wait_recv()
    share_sum = share[z, c, x].astype(jnp.float32) + x_in[z].astype(jnp.float32)
    out_sum = stream_in[...] + share_sum
    stream_ref[...] = out_sum

    @pl.when(z > 0)
    def _():
        chain_copy(z, z, z).wait_recv()
        stream_ref[...] += chain_in[z].astype(jnp.float32)

    @pl.when(z < 3)
    def _():
        chain_copy(z, z, 4).wait_recv()
        stream_ref[...] += chain_in[4].astype(jnp.float32)

    out_ref[...] = stream_ref[...].astype(out_ref.dtype)

    def settle(p, carry):
        pl.when((p <= z) & (z < 3))(lambda: up_copy(p).wait_send())
        pl.when((p >= z) & (z > 0))(lambda: down_copy(p).wait_send())
        x_copy(p).wait_send()
        core_copy(p, 0).wait_send()
        core_copy(p, 1).wait_send()
        pair_copy(p).wait_send()
        half_copy(p).wait_send()
        send_chain(p, lambda copy: copy.wait_send())
        return carry

    lax.fori_loop(0, 4, settle, 0)


def exchange(own, stream, expert_weight):
    block_rows, width = stream.shape
    wide = own.shape[1]
    units = expert_weight.shape[2]
    vmem = pl.BlockSpec(memory_space=pltpu.VMEM)
    rows_all = 16 * block_rows
    dma = pltpu.SemaphoreType.DMA
    return pl.pallas_call(
        moe_kernel,
        out_shape=jax.ShapeDtypeStruct((block_rows, width), jnp.bfloat16),
        in_specs=[vmem, vmem, pl.BlockSpec(memory_space=pl.ANY)],
        out_specs=vmem,
        scratch_shapes=[
            pltpu.VMEM((4, 4 * block_rows, wide), jnp.bfloat16),
            pltpu.VMEM((width, units), jnp.bfloat16),
            pltpu.VMEM((block_rows, width), jnp.float32),
            pltpu.VMEM((4, 2, 2, block_rows, width), jnp.bfloat16),
            pltpu.VMEM((4 * block_rows, units), jnp.bfloat16),
            pltpu.VMEM((4, 2, block_rows, width), jnp.bfloat16),
            pltpu.VMEM((4, block_rows, width), jnp.bfloat16),
            pltpu.VMEM((5, block_rows, width), jnp.bfloat16),
            dma, dma, dma((2, 4)), dma((4,)), dma((4, 2)), dma((16,)),
            dma((4,)), dma((4,)), dma((4,)), dma((4,)), dma((4,)), dma((5,)),
        ],
        compiler_params=pltpu.CompilerParams(
            collective_id=0, has_side_effects=True, vmem_limit_bytes=56 * 1024 * 1024
        ),
        cost_estimate=pl.CostEstimate(
            flops=4 * rows_all * width * units,
            bytes_accessed=2 * width * units + 16 * block_rows * width,
            transcendentals=rows_all * units,
        ),
    )(own, stream, expert_weight)


def local_dense(residual, attn_partial, norm_gain, router_weight, expert_ids, expert_weight):
    stream, gates, restored = local_rows(
        residual, attn_partial, norm_gain, router_weight, expert_ids
    )
    expert_count = gates.shape[1]
    high = gates.astype(jnp.bfloat16)
    low = (gates - high.astype(jnp.float32)).astype(jnp.bfloat16)
    spare = jnp.zeros((gates.shape[0], 64 - expert_count), jnp.bfloat16)
    own = jnp.concatenate([restored, high, spare, low, spare], axis=1)
    return exchange(own, stream, expert_weight)


def dense_fits(mesh, row_count, expert_count, top_count):
    return (
        mesh.shape["tensor"] == 1
        and mesh.shape["expert"] == expert_count == 16
        and expert_count <= 4 * top_count
    )


def solution(mesh):
    placed = (
        P(("group", "expert"), "tensor"),
        P("tensor", ("group", "expert"), None),
        P(),
        P("tensor", None),
        P(("group", "expert"), None),
        P("expert", None, "tensor"),
    )

    def run(residual, attn_partial, norm_gain, router_weight, expert_ids, expert_weight):
        dense = dense_fits(mesh, residual.shape[0], router_weight.shape[1], expert_ids.shape[1])
        return jax.shard_map(
            local_dense if dense else local,
            mesh=mesh,
            in_specs=placed,
            out_specs=P(("group", "expert"), "tensor"),
            check_vma=False,
        )(residual, attn_partial, norm_gain, router_weight, expert_ids, expert_weight)

    return run
```

```python
import jax
import jax.numpy as jnp
from jax import lax
from jax.experimental import pallas as pl
from jax.experimental.pallas import tpu as pltpu
from jax.sharding import PartitionSpec as P

QBLOCK = 128


EPS = 1e-06
ROUTE_SCALE = 2.5


def encode(values):
    row_count, columns = values.shape
    blocks = values.astype(jnp.float32).reshape(row_count, columns // QBLOCK, QBLOCK)
    largest = jnp.max(jnp.abs(blocks), axis=-1)
    block_scale = ((largest + EPS) / 448.0).astype(jnp.bfloat16)
    encoded = (blocks / block_scale.astype(jnp.float32)[:, :, None]).astype(jnp.bfloat16)
    return (encoded.reshape(row_count, columns), block_scale)


def decode(encoded, block_scale):
    leading = encoded.shape[:-1]
    columns = encoded.shape[-1]
    blocks = encoded.astype(jnp.float32).reshape(leading + (columns // QBLOCK, QBLOCK))
    restored = (blocks * block_scale.astype(jnp.float32)[..., None]).astype(jnp.bfloat16)
    return restored.reshape(leading + (columns,))


def local(residual, attn_partial, norm_gain, router_weight, expert_ids, expert_weight):
    row_count, share_width = residual.shape
    tensor_count = lax.axis_size("tensor")
    model_width = share_width * tensor_count
    expert_count = router_weight.shape[1]
    top_count = expert_ids.shape[1]
    capacity = min(row_count, max(2, 7 * row_count * top_count // (4 * expert_count)))
    first_column = lax.axis_index("tensor") * share_width
    partial_attn = attn_partial[0].astype(jnp.float32)
    full_residual = lax.all_gather(residual, "tensor", axis=1, tiled=True)
    attention = lax.psum(partial_attn.astype(jnp.bfloat16), "tensor").astype(jnp.float32)
    stream = full_residual.astype(jnp.float32) + attention
    meansq = jnp.mean(stream * stream, axis=1, keepdims=True)
    normed = (stream * lax.rsqrt(meansq + EPS) * norm_gain).astype(jnp.bfloat16)
    normed_share = lax.dynamic_slice_in_dim(normed, first_column, share_width, 1)
    stream_share = lax.dynamic_slice_in_dim(stream, first_column, share_width, 1)
    logits = lax.psum(
        jnp.dot(normed_share, router_weight, preferred_element_type=jnp.float32).astype(
            jnp.bfloat16
        ),
        "tensor",
    ).astype(jnp.float32)
    affinity = jax.nn.sigmoid(logits)
    chosen = expert_ids[:, :, None] == jnp.arange(expert_count, dtype=jnp.int32)[None, None, :]
    picked = jnp.sum(jnp.where(chosen, affinity[:, None, :], 0.0), axis=2)
    gate_values = ROUTE_SCALE * picked / jnp.sum(picked, axis=1, keepdims=True)
    encoded, block_scale = encode(normed)
    flat_ids = expert_ids.reshape(-1)
    onehot = (flat_ids[:, None] == jnp.arange(expert_count, dtype=jnp.int32)[None, :]).astype(
        jnp.int32
    )
    before = jnp.cumsum(onehot, axis=0) - onehot
    slot_index = jnp.sum(before * onehot, axis=1)
    target_slot = flat_ids * capacity + slot_index
    source_row = jnp.arange(row_count * top_count, dtype=jnp.int32) // top_count
    send_codes = (
        jnp.zeros((expert_count * capacity, encoded.shape[1]), jnp.bfloat16)
        .at[target_slot]
        .set(encoded[source_row])
    )
    send_scales = (
        jnp.zeros((expert_count * capacity, block_scale.shape[1]), jnp.bfloat16)
        .at[target_slot]
        .set(block_scale[source_row])
    )
    send_codes = send_codes.reshape(expert_count, 1, capacity, encoded.shape[1])
    send_scales = send_scales.reshape(expert_count, 1, capacity, block_scale.shape[1])
    codes_in = lax.all_to_all(send_codes, "expert", split_axis=0, concat_axis=1, tiled=True)
    scales_in = lax.all_to_all(send_scales, "expert", split_axis=0, concat_axis=1, tiled=True)
    inputs = decode(codes_in, scales_in)
    leading = inputs.shape[:-1]
    flat_rows = inputs.reshape(-1, model_width)
    w_expert = expert_weight[0]
    hidden = jax.nn.silu(jnp.dot(flat_rows, w_expert, preferred_element_type=jnp.float32)).astype(
        jnp.bfloat16
    )
    output = lax.dot_general(
        hidden, w_expert, (((1,), (1,)), ((), ())), preferred_element_type=jnp.float32
    ).astype(jnp.bfloat16)
    halves = output.reshape(leading + (tensor_count, 1, share_width))
    returned = lax.all_to_all(
        lax.all_to_all(halves, "expert", split_axis=1, concat_axis=0, tiled=True),
        "tensor",
        split_axis=3,
        concat_axis=4,
        tiled=True,
    )
    expert_out = jnp.sum(returned.astype(jnp.float32), axis=(3, 4)).astype(jnp.bfloat16)
    taken = expert_out.reshape(expert_count * capacity, share_width)[target_slot]
    taken = taken.reshape(row_count, top_count, share_width)
    moe_share = jnp.einsum("rk,rkd->rd", gate_values, taken.astype(jnp.float32))
    return (stream_share + moe_share).astype(jnp.bfloat16)


def moe_kernel(residual_ref, attn_ref, gain_ref, router_ref, ids_ref, weight_hbm, out_ref, rows, weight, stream_ref, stage, share, hidden, core_in, x_in,
               chain_in, weight_sem, line_send, x_send, core_send, row_recv,
               pair_send, pair_recv, half_send, half_recv, chain_send, chain_recv):
    block_rows, width = out_ref.shape
    tile = 256
    me = lax.axis_index("expert")
    z, x, c = me // 4, (me // 2) % 2, me % 2
    flip = z // 2
    m = z + flip * (3 - 2 * z)

    def expert_at(zz, xx, cc):
        return (zz * 2 + xx) * 2 + cc

    def place(o):
        return o + flip * (3 - 2 * o)

    def to(zz, xx, cc):
        return {"expert": expert_at(zz, xx, cc)}

    def slot(zz, xx, cc):
        return rows.at[zz, pl.ds(pl.multiple_of(block_rows * (2 * xx + cc), block_rows), block_rows), :]

    barrier = pltpu.get_barrier_semaphore()

    def greet(device):
        pl.semaphore_signal(barrier, inc=1, device_id=device, device_id_type=pl.DeviceIdType.MESH)

    load_weight = pltpu.make_async_copy(weight_hbm.at[0], weight, weight_sem)
    load_weight.start()
    greet(to(z, 1 - x, c))
    greet(to(z, x, 1 - c))
    pl.when(z > 0)(lambda: greet(to(z - 1, x, c)))
    pl.when(z < 3)(lambda: greet(to(z + 1, x, c)))
    stream = residual_ref[...].astype(jnp.float32) + attn_ref[0].astype(jnp.float32)
    stream_ref[...] = stream
    meansq = jnp.sum(stream * stream, axis=1, keepdims=True) * (1.0 / width)
    inverse = lax.rsqrt(meansq + EPS)
    own = pl.ds(pl.multiple_of(block_rows * (2 * x + c), block_rows), block_rows)
    expert_count = router_ref.shape[1]
    for b in range(width // QBLOCK):
        cols = slice(b * QBLOCK, (b + 1) * QBLOCK)
        normed = (stream_ref[:, cols] * inverse * gain_ref[:, cols]).astype(jnp.bfloat16)
        rows[z, own, cols] = normed
        values = normed.astype(jnp.float32)
        largest = jnp.max(jnp.abs(values), axis=1, keepdims=True)
        scale = ((largest + EPS) / 448.0).astype(jnp.bfloat16).astype(jnp.float32)
        encoded = (values / scale).astype(jnp.bfloat16)
        stage[:, cols] = (encoded.astype(jnp.float32) * scale).astype(jnp.bfloat16)
    logits = jnp.dot(
        rows[z, own, :width], router_ref[...], preferred_element_type=jnp.float32
    )
    rows[z, own, :width] = stage[...]
    affinity = 1.0 / (1.0 + jnp.exp(-logits))
    expert = lax.broadcasted_iota(jnp.int32, logits.shape, 1)
    picked = jnp.zeros_like(affinity)
    for j in range(ids_ref.shape[1]):
        picked += jnp.where(ids_ref[:, j:j + 1] == expert, affinity, 0.0)
    gates = ROUTE_SCALE * picked / jnp.sum(picked, axis=1, keepdims=True)
    high = gates.astype(jnp.bfloat16).astype(jnp.float32)
    spare = jnp.zeros((block_rows, 64 - expert_count), jnp.float32)
    wide_gates = jnp.concatenate([high, spare, gates - high, spare], axis=1)
    rows[z, own, width:] = wide_gates.astype(jnp.bfloat16)
    pl.semaphore_wait(barrier, 3 + m)

    def row_copy(zz, xx, cc, sem, device):
        part = slot(zz, xx, cc)
        return pltpu.make_async_remote_copy(
            src_ref=part, dst_ref=part, send_sem=sem, recv_sem=row_recv.at[expert_at(zz, xx, cc)],
            device_id=device, device_id_type=pl.DeviceIdType.MESH,
        )

    def up_copy(p):
        return row_copy(p, x, c, line_send.at[0, p], to(z + 1, x, c))

    def down_copy(p):
        return row_copy(p, x, c, line_send.at[1, p], to(z - 1, x, c))

    def x_copy(p):
        return row_copy(p, x, c, x_send.at[p], to(z, 1 - x, c))

    def core_copy(p, xx):
        return row_copy(p, xx, c, core_send.at[p, xx], to(z, x, 1 - c))

    def got(zz, xx, cc):
        row_copy(zz, xx, cc, x_send.at[0], to(z, 1 - x, c)).wait_recv()

    def pass_on(p):
        pl.when((p <= z) & (z < 3))(lambda: up_copy(p).start())
        pl.when((p >= z) & (z > 0))(lambda: down_copy(p).start())
        x_copy(p).start()
        core_copy(p, x).start()

    def arrive_line(p):
        got(p, x, c)
        pass_on(p)

    def pair_copy(p):
        return pltpu.make_async_remote_copy(
            src_ref=share.at[p, 1 - c], dst_ref=core_in.at[p],
            send_sem=pair_send.at[p], recv_sem=pair_recv.at[p],
            device_id=to(z, x, 1 - c), device_id_type=pl.DeviceIdType.MESH,
        )

    def half_copy(p):
        return pltpu.make_async_remote_copy(
            src_ref=share.at[p, c, 1 - x], dst_ref=x_in.at[p],
            send_sem=half_send.at[p], recv_sem=half_recv.at[p],
            device_id=to(z, 1 - x, c), device_id_type=pl.DeviceIdType.MESH,
        )

    def chain_copy(p, towards, index):
        return pltpu.make_async_remote_copy(
            src_ref=share.at[p, c, x], dst_ref=chain_in.at[index],
            send_sem=chain_send.at[p], recv_sem=chain_recv.at[index],
            device_id=to(towards, x, c), device_id_type=pl.DeviceIdType.MESH,
        )

    def send_chain(p, act):
        pl.when(p > z)(lambda: act(chain_copy(p, z + 1, p)))
        pl.when(p == z - 1)(lambda: act(chain_copy(p, z - 1, 4)))
        pl.when(p < z - 1)(lambda: act(chain_copy(p, z - 1, p)))

    def compute(p):
        units = weight.shape[1]
        gate_block = rows[p, :, width:].astype(jnp.float32)
        lane = lax.broadcasted_iota(jnp.int32, gate_block.shape, 1)
        mine = (lane == me) | (lane == me + 64)
        gate = jnp.sum(jnp.where(mine, gate_block, 0.0), axis=1, keepdims=True)

        def first(n, carry):
            columns = pl.ds(pl.multiple_of(n * tile, tile), tile)
            v = jnp.dot(rows[p, :, :width], weight[:, columns], preferred_element_type=jnp.float32)
            hidden[:, columns] = (v / (1.0 + jnp.exp(-v))).astype(jnp.bfloat16)
            return carry

        lax.fori_loop(0, units // tile, first, 0)

        def second(n, carry):
            columns = pl.ds(pl.multiple_of(n * tile, tile), tile)
            v = lax.dot_general(
                hidden[...], weight[columns, :], (((1,), (1,)), ((), ())),
                preferred_element_type=jnp.float32,
            )
            v = v.astype(jnp.bfloat16).astype(jnp.float32) * gate
            v = v.astype(jnp.bfloat16)
            for i in range(4):
                share[p, i % 2, i // 2, :, columns] = v[i * block_rows:(i + 1) * block_rows]
            return carry

        lax.fori_loop(0, width // tile, second, 0)

    def add_pair(p):
        pair_copy(p).wait_recv()
        for xx in range(2):
            share[p, c, xx] = (
                share[p, c, xx].astype(jnp.float32) + core_in[p, xx].astype(jnp.float32)
            ).astype(jnp.bfloat16)
        half_copy(p).start()

    def add_half(p):
        half_copy(p).wait_recv()
        has = ((p > z) & (z > 0)) | ((p < z) & (z < 3))

        @pl.when(has)
        def _():
            chain_copy(p, z, p).wait_recv()
            share[p, c, x] = (
                share[p, c, x].astype(jnp.float32) + x_in[p].astype(jnp.float32)
                + chain_in[p].astype(jnp.float32)
            ).astype(jnp.bfloat16)

        @pl.when(jnp.logical_not(has))
        def _():
            share[p, c, x] = (
                share[p, c, x].astype(jnp.float32) + x_in[p].astype(jnp.float32)
            ).astype(jnp.bfloat16)

        send_chain(p, lambda copy: copy.start())

    pass_on(z)
    middle = m == 1

    def step(k, carry):
        own_order = jnp.where(k == 0, m, jnp.where(k == 1, 1 - m, k))
        p = place(own_order)
        later = place(jnp.where(k == 0, 1 - m, k + 1))
        pl.when(k < 3 - 2 * m)(lambda: arrive_line(later))
        pl.when(middle & (k == 0))(lambda: arrive_line(place(2)))
        pl.when(middle & (k == 1))(lambda: arrive_line(place(3)))
        got(p, 1 - x, c)
        core_copy(p, 1 - x).start()
        pl.when(k == 3)(lambda: add_pair(place(2)))
        got(p, x, 1 - c)
        got(p, 1 - x, 1 - c)
        pl.when(k == 0)(lambda: load_weight.wait())
        compute(p)
        pair_copy(p).start()
        return carry

    lax.fori_loop(0, 4, step, 0)

    order = [place(2), place(3), place(1 - m), z]
    add_pair(order[1])
    add_half(order[0])
    add_pair(order[2])
    add_half(order[1])
    add_pair(order[3])
    add_half(order[2])
    half_copy(z).wait_recv()
    share_sum = share[z, c, x].astype(jnp.float32) + x_in[z].astype(jnp.float32)
    out_sum = stream_ref[...] + share_sum
    stream_ref[...] = out_sum

    @pl.when(z > 0)
    def _():
        chain_copy(z, z, z).wait_recv()
        stream_ref[...] += chain_in[z].astype(jnp.float32)

    @pl.when(z < 3)
    def _():
        chain_copy(z, z, 4).wait_recv()
        stream_ref[...] += chain_in[4].astype(jnp.float32)

    out_ref[...] = stream_ref[...].astype(out_ref.dtype)

    def settle(p, carry):
        pl.when((p <= z) & (z < 3))(lambda: up_copy(p).wait_send())
        pl.when((p >= z) & (z > 0))(lambda: down_copy(p).wait_send())
        x_copy(p).wait_send()
        core_copy(p, 0).wait_send()
        core_copy(p, 1).wait_send()
        pair_copy(p).wait_send()
        half_copy(p).wait_send()
        send_chain(p, lambda copy: copy.wait_send())
        return carry

    lax.fori_loop(0, 4, settle, 0)


def exchange(residual, attn_partial, norm_gain, router_weight, expert_ids, expert_weight):
    block_rows, width = residual.shape
    wide = width + 128
    units = expert_weight.shape[2]
    vmem = pl.BlockSpec(memory_space=pltpu.VMEM)
    rows_all = 16 * block_rows
    dma = pltpu.SemaphoreType.DMA
    return pl.pallas_call(
        moe_kernel,
        out_shape=jax.ShapeDtypeStruct((block_rows, width), jnp.bfloat16),
        in_specs=[vmem] * 5 + [pl.BlockSpec(memory_space=pl.ANY)],
        out_specs=vmem,
        scratch_shapes=[
            pltpu.VMEM((4, 4 * block_rows, wide), jnp.bfloat16),
            pltpu.VMEM((width, units), jnp.bfloat16),
            pltpu.VMEM((block_rows, width), jnp.float32),
            pltpu.VMEM((block_rows, width), jnp.bfloat16),
            pltpu.VMEM((4, 2, 2, block_rows, width), jnp.bfloat16),
            pltpu.VMEM((4 * block_rows, units), jnp.bfloat16),
            pltpu.VMEM((4, 2, block_rows, width), jnp.bfloat16),
            pltpu.VMEM((4, block_rows, width), jnp.bfloat16),
            pltpu.VMEM((5, block_rows, width), jnp.bfloat16),
            dma, dma((2, 4)), dma((4,)), dma((4, 2)), dma((16,)),
            dma((4,)), dma((4,)), dma((4,)), dma((4,)), dma((4,)), dma((5,)),
        ],
        compiler_params=pltpu.CompilerParams(
            collective_id=0, has_side_effects=True, vmem_limit_bytes=56 * 1024 * 1024
        ),
        cost_estimate=pl.CostEstimate(
            flops=4 * rows_all * width * units,
            bytes_accessed=2 * width * units + 16 * block_rows * width,
            transcendentals=rows_all * units,
        ),
    )(residual, attn_partial, norm_gain[None, :], router_weight, expert_ids, expert_weight)


def dense_fits(mesh, row_count, expert_count, top_count):
    return (
        mesh.shape["tensor"] == 1
        and mesh.shape["expert"] == expert_count == 16
        and expert_count <= 4 * top_count
    )


def solution(mesh):
    placed = (
        P(("group", "expert"), "tensor"),
        P("tensor", ("group", "expert"), None),
        P(),
        P("tensor", None),
        P(("group", "expert"), None),
        P("expert", None, "tensor"),
    )

    def run(residual, attn_partial, norm_gain, router_weight, expert_ids, expert_weight):
        dense = dense_fits(mesh, residual.shape[0], router_weight.shape[1], expert_ids.shape[1])
        return jax.shard_map(
            exchange if dense else local,
            mesh=mesh,
            in_specs=placed,
            out_specs=P(("group", "expert"), "tensor"),
            check_vma=False,
        )(residual, attn_partial, norm_gain, router_weight, expert_ids, expert_weight)

    return run
```

```python
import jax
import jax.numpy as jnp
from jax import lax
from jax.experimental import pallas as pl
from jax.experimental.pallas import tpu as pltpu
from jax.sharding import PartitionSpec as P

QBLOCK = 128


EPS = 1e-06
ROUTE_SCALE = 2.5


def encode(values):
    row_count, columns = values.shape
    blocks = values.astype(jnp.float32).reshape(row_count, columns // QBLOCK, QBLOCK)
    largest = jnp.max(jnp.abs(blocks), axis=-1)
    block_scale = ((largest + EPS) / 448.0).astype(jnp.bfloat16)
    encoded = (blocks / block_scale.astype(jnp.float32)[:, :, None]).astype(jnp.bfloat16)
    return (encoded.reshape(row_count, columns), block_scale)


def decode(encoded, block_scale):
    leading = encoded.shape[:-1]
    columns = encoded.shape[-1]
    blocks = encoded.astype(jnp.float32).reshape(leading + (columns // QBLOCK, QBLOCK))
    restored = (blocks * block_scale.astype(jnp.float32)[..., None]).astype(jnp.bfloat16)
    return restored.reshape(leading + (columns,))


def local(residual, attn_partial, norm_gain, router_weight, expert_ids, expert_weight):
    row_count, share_width = residual.shape
    tensor_count = lax.axis_size("tensor")
    model_width = share_width * tensor_count
    expert_count = router_weight.shape[1]
    top_count = expert_ids.shape[1]
    capacity = min(row_count, max(2, 7 * row_count * top_count // (4 * expert_count)))
    first_column = lax.axis_index("tensor") * share_width
    partial_attn = attn_partial[0].astype(jnp.float32)
    full_residual = lax.all_gather(residual, "tensor", axis=1, tiled=True)
    attention = lax.psum(partial_attn.astype(jnp.bfloat16), "tensor").astype(jnp.float32)
    stream = full_residual.astype(jnp.float32) + attention
    meansq = jnp.mean(stream * stream, axis=1, keepdims=True)
    normed = (stream * lax.rsqrt(meansq + EPS) * norm_gain).astype(jnp.bfloat16)
    normed_share = lax.dynamic_slice_in_dim(normed, first_column, share_width, 1)
    stream_share = lax.dynamic_slice_in_dim(stream, first_column, share_width, 1)
    logits = lax.psum(
        jnp.dot(normed_share, router_weight, preferred_element_type=jnp.float32).astype(
            jnp.bfloat16
        ),
        "tensor",
    ).astype(jnp.float32)
    affinity = jax.nn.sigmoid(logits)
    chosen = expert_ids[:, :, None] == jnp.arange(expert_count, dtype=jnp.int32)[None, None, :]
    picked = jnp.sum(jnp.where(chosen, affinity[:, None, :], 0.0), axis=2)
    gate_values = ROUTE_SCALE * picked / jnp.sum(picked, axis=1, keepdims=True)
    encoded, block_scale = encode(normed)
    flat_ids = expert_ids.reshape(-1)
    onehot = (flat_ids[:, None] == jnp.arange(expert_count, dtype=jnp.int32)[None, :]).astype(
        jnp.int32
    )
    before = jnp.cumsum(onehot, axis=0) - onehot
    slot_index = jnp.sum(before * onehot, axis=1)
    target_slot = flat_ids * capacity + slot_index
    source_row = jnp.arange(row_count * top_count, dtype=jnp.int32) // top_count
    send_codes = (
        jnp.zeros((expert_count * capacity, encoded.shape[1]), jnp.bfloat16)
        .at[target_slot]
        .set(encoded[source_row])
    )
    send_scales = (
        jnp.zeros((expert_count * capacity, block_scale.shape[1]), jnp.bfloat16)
        .at[target_slot]
        .set(block_scale[source_row])
    )
    send_codes = send_codes.reshape(expert_count, 1, capacity, encoded.shape[1])
    send_scales = send_scales.reshape(expert_count, 1, capacity, block_scale.shape[1])
    codes_in = lax.all_to_all(send_codes, "expert", split_axis=0, concat_axis=1, tiled=True)
    scales_in = lax.all_to_all(send_scales, "expert", split_axis=0, concat_axis=1, tiled=True)
    inputs = decode(codes_in, scales_in)
    leading = inputs.shape[:-1]
    flat_rows = inputs.reshape(-1, model_width)
    w_expert = expert_weight[0]
    hidden = jax.nn.silu(jnp.dot(flat_rows, w_expert, preferred_element_type=jnp.float32)).astype(
        jnp.bfloat16
    )
    output = lax.dot_general(
        hidden, w_expert, (((1,), (1,)), ((), ())), preferred_element_type=jnp.float32
    ).astype(jnp.bfloat16)
    halves = output.reshape(leading + (tensor_count, 1, share_width))
    returned = lax.all_to_all(
        lax.all_to_all(halves, "expert", split_axis=1, concat_axis=0, tiled=True),
        "tensor",
        split_axis=3,
        concat_axis=4,
        tiled=True,
    )
    expert_out = jnp.sum(returned.astype(jnp.float32), axis=(3, 4)).astype(jnp.bfloat16)
    taken = expert_out.reshape(expert_count * capacity, share_width)[target_slot]
    taken = taken.reshape(row_count, top_count, share_width)
    moe_share = jnp.einsum("rk,rkd->rd", gate_values, taken.astype(jnp.float32))
    return (stream_share + moe_share).astype(jnp.bfloat16)


def moe_kernel(residual_ref, attn_ref, gain_ref, router_ref, ids_ref, weight_hbm, out_ref, rows, weight, stream_ref, stage, share, hidden, core_in, x_in,
               chain_in, weight_sem, line_send, x_send, core_send, row_recv,
               pair_send, pair_recv, half_send, half_recv, chain_send, chain_recv):
    block_rows, width = out_ref.shape
    tile = 256
    me = lax.axis_index("expert")
    z, x, c = me // 4, (me // 2) % 2, me % 2
    flip = z // 2
    m = z + flip * (3 - 2 * z)

    def expert_at(zz, xx, cc):
        return (zz * 2 + xx) * 2 + cc

    def place(o):
        return o + flip * (3 - 2 * o)

    def to(zz, xx, cc):
        return {"expert": expert_at(zz, xx, cc)}

    def slot(zz, xx, cc):
        return rows.at[zz, pl.ds(pl.multiple_of(block_rows * (2 * xx + cc), block_rows), block_rows), :]

    barrier = pltpu.get_barrier_semaphore()

    def greet(device):
        pl.semaphore_signal(barrier, inc=1, device_id=device, device_id_type=pl.DeviceIdType.MESH)

    load_weight = pltpu.make_async_copy(weight_hbm.at[0], weight, weight_sem)
    load_weight.start()
    greet(to(z, 1 - x, c))
    greet(to(z, x, 1 - c))
    pl.when(z > 0)(lambda: greet(to(z - 1, x, c)))
    pl.when(z < 3)(lambda: greet(to(z + 1, x, c)))
    stream = residual_ref[...].astype(jnp.float32) + attn_ref[0].astype(jnp.float32)
    stream_ref[...] = stream
    meansq = jnp.sum(stream * stream, axis=1, keepdims=True) * (1.0 / width)
    inverse = lax.rsqrt(meansq + EPS)
    own = pl.ds(pl.multiple_of(block_rows * (2 * x + c), block_rows), block_rows)
    expert_count = router_ref.shape[1]
    for b in range(width // QBLOCK):
        cols = slice(b * QBLOCK, (b + 1) * QBLOCK)
        normed = (stream_ref[:, cols] * inverse * gain_ref[:, cols]).astype(jnp.bfloat16)
        rows[z, own, cols] = normed
        values = normed.astype(jnp.float32)
        largest = jnp.max(jnp.abs(values), axis=1, keepdims=True)
        scale = ((largest + EPS) / 448.0).astype(jnp.bfloat16).astype(jnp.float32)
        encoded = (values / scale).astype(jnp.bfloat16)
        stage[:, cols] = (encoded.astype(jnp.float32) * scale).astype(jnp.bfloat16)
    logits = jnp.dot(
        rows[z, own, :width], router_ref[...], preferred_element_type=jnp.float32
    )
    rows[z, own, :width] = stage[...]
    affinity = 1.0 / (1.0 + jnp.exp(-logits))
    expert = lax.broadcasted_iota(jnp.int32, logits.shape, 1)
    picked = jnp.zeros_like(affinity)
    for j in range(ids_ref.shape[1]):
        picked += jnp.where(ids_ref[:, j:j + 1] == expert, affinity, 0.0)
    gates = ROUTE_SCALE * picked / jnp.sum(picked, axis=1, keepdims=True)
    high = gates.astype(jnp.bfloat16).astype(jnp.float32)
    spare = jnp.zeros((block_rows, 64 - expert_count), jnp.float32)
    wide_gates = jnp.concatenate([high, spare, gates - high, spare], axis=1)
    rows[z, own, width:] = wide_gates.astype(jnp.bfloat16)
    pl.semaphore_wait(barrier, 3 + m)

    def row_copy(zz, xx, cc, sem, device):
        part = slot(zz, xx, cc)
        return pltpu.make_async_remote_copy(
            src_ref=part, dst_ref=part, send_sem=sem, recv_sem=row_recv.at[expert_at(zz, xx, cc)],
            device_id=device, device_id_type=pl.DeviceIdType.MESH,
        )

    def up_copy(p):
        return row_copy(p, x, c, line_send.at[0, p], to(z + 1, x, c))

    def down_copy(p):
        return row_copy(p, x, c, line_send.at[1, p], to(z - 1, x, c))

    def x_copy(p):
        return row_copy(p, x, c, x_send.at[p], to(z, 1 - x, c))

    def core_copy(p, xx):
        return row_copy(p, xx, c, core_send.at[p, xx], to(z, x, 1 - c))

    def got(zz, xx, cc):
        row_copy(zz, xx, cc, x_send.at[0], to(z, 1 - x, c)).wait_recv()

    def pass_on(p):
        pl.when((p <= z) & (z < 3))(lambda: up_copy(p).start())
        pl.when((p >= z) & (z > 0))(lambda: down_copy(p).start())
        x_copy(p).start()
        core_copy(p, x).start()

    def arrive_line(p):
        got(p, x, c)
        pass_on(p)

    half = width // 256 * 128

    def piece(h):
        return pl.ds(0, half) if h == 0 else pl.ds(half, width - half)

    def pair_copy(p):
        return pltpu.make_async_remote_copy(
            src_ref=share.at[p, 1 - c], dst_ref=core_in.at[p],
            send_sem=pair_send.at[p], recv_sem=pair_recv.at[p],
            device_id=to(z, x, 1 - c), device_id_type=pl.DeviceIdType.MESH,
        )

    def half_copy(p, h):
        return pltpu.make_async_remote_copy(
            src_ref=share.at[p, c, 1 - x, :, piece(h)], dst_ref=x_in.at[p, :, piece(h)],
            send_sem=half_send.at[h, p], recv_sem=half_recv.at[h, p],
            device_id=to(z, 1 - x, c), device_id_type=pl.DeviceIdType.MESH,
        )

    def chain_copy(p, towards, index, h):
        return pltpu.make_async_remote_copy(
            src_ref=share.at[p, c, x, :, piece(h)], dst_ref=chain_in.at[index, :, piece(h)],
            send_sem=chain_send.at[h, p], recv_sem=chain_recv.at[h, index],
            device_id=to(towards, x, c), device_id_type=pl.DeviceIdType.MESH,
        )

    def send_chain(p, h, act):
        pl.when(p > z)(lambda: act(chain_copy(p, z + 1, p, h)))
        pl.when(p == z - 1)(lambda: act(chain_copy(p, z - 1, 4, h)))
        pl.when(p < z - 1)(lambda: act(chain_copy(p, z - 1, p, h)))

    def compute(p):
        units = weight.shape[1]
        gate_block = rows[p, :, width:].astype(jnp.float32)
        lane = lax.broadcasted_iota(jnp.int32, gate_block.shape, 1)
        mine = (lane == me) | (lane == me + 64)
        gate = jnp.sum(jnp.where(mine, gate_block, 0.0), axis=1, keepdims=True)

        def first(n, carry):
            columns = pl.ds(pl.multiple_of(n * tile, tile), tile)
            v = jnp.dot(rows[p, :, :width], weight[:, columns], preferred_element_type=jnp.float32)
            hidden[:, columns] = (v / (1.0 + jnp.exp(-v))).astype(jnp.bfloat16)
            return carry

        lax.fori_loop(0, units // tile, first, 0)

        def second(n, carry):
            columns = pl.ds(pl.multiple_of(n * tile, tile), tile)
            v = lax.dot_general(
                hidden[...], weight[columns, :], (((1,), (1,)), ((), ())),
                preferred_element_type=jnp.float32,
            )
            v = v.astype(jnp.bfloat16).astype(jnp.float32) * gate
            v = v.astype(jnp.bfloat16)
            for i in range(4):
                share[p, i % 2, i // 2, :, columns] = v[i * block_rows:(i + 1) * block_rows]
            return carry

        lax.fori_loop(0, width // tile, second, 0)

    def add_pair(p):
        pair_copy(p).wait_recv()
        share[p, c, 1 - x] = (
            share[p, c, 1 - x].astype(jnp.float32) + core_in[p, 1 - x].astype(jnp.float32)
        ).astype(jnp.bfloat16)
        half_copy(p, 0).start()
        half_copy(p, 1).start()

    def add_half(p, h):
        cols = piece(h)
        half_copy(p, h).wait_recv()
        has = ((p > z) & (z > 0)) | ((p < z) & (z < 3))

        def total():
            return (
                share[p, c, x, :, cols].astype(jnp.float32)
                + core_in[p, x, :, cols].astype(jnp.float32)
                + x_in[p, :, cols].astype(jnp.float32)
            )

        @pl.when(has)
        def _():
            chain_copy(p, z, p, h).wait_recv()
            share[p, c, x, :, cols] = (
                total() + chain_in[p, :, cols].astype(jnp.float32)
            ).astype(jnp.bfloat16)

        @pl.when(jnp.logical_not(has))
        def _():
            share[p, c, x, :, cols] = total().astype(jnp.bfloat16)

        send_chain(p, h, lambda copy: copy.start())

    pass_on(z)
    middle = m == 1

    def step(k, carry):
        own_order = jnp.where(k == 0, m, jnp.where(k == 1, 1 - m, k))
        p = place(own_order)
        later = place(jnp.where(k == 0, 1 - m, k + 1))
        pl.when(k < 3 - 2 * m)(lambda: arrive_line(later))
        pl.when(middle & (k == 0))(lambda: arrive_line(place(2)))
        pl.when(middle & (k == 1))(lambda: arrive_line(place(3)))
        got(p, 1 - x, c)
        core_copy(p, 1 - x).start()
        pl.when(k == 3)(lambda: add_pair(place(2)))
        got(p, x, 1 - c)
        got(p, 1 - x, 1 - c)
        pl.when(k == 0)(lambda: load_weight.wait())
        compute(p)
        pair_copy(p).start()
        return carry

    lax.fori_loop(0, 4, step, 0)

    order = [place(2), place(3), place(1 - m), z]
    add_pair(order[1])
    add_half(order[0], 0)
    add_half(order[0], 1)
    add_pair(order[2])
    add_half(order[1], 0)
    add_half(order[1], 1)
    add_pair(order[3])
    add_half(order[2], 0)
    add_half(order[2], 1)
    for h in range(2):
        cols = piece(h)
        half_copy(z, h).wait_recv()
        stream_ref[:, cols] += (
            share[z, c, x, :, cols].astype(jnp.float32)
            + core_in[z, x, :, cols].astype(jnp.float32)
            + x_in[z, :, cols].astype(jnp.float32)
        )

    for h in range(2):
        cols = piece(h)

        def add_chain(index, cols=cols, h=h):
            chain_copy(z, z, index, h).wait_recv()
            stream_ref[:, cols] += chain_in[index, :, cols].astype(jnp.float32)

        pl.when(z > 0)(lambda f=add_chain: f(z))
        pl.when(z < 3)(lambda f=add_chain: f(4))
        out_ref[:, cols] = stream_ref[:, cols].astype(out_ref.dtype)

    def settle(p, carry):
        pl.when((p <= z) & (z < 3))(lambda: up_copy(p).wait_send())
        pl.when((p >= z) & (z > 0))(lambda: down_copy(p).wait_send())
        x_copy(p).wait_send()
        core_copy(p, 0).wait_send()
        core_copy(p, 1).wait_send()
        pair_copy(p).wait_send()
        for h in range(2):
            half_copy(p, h).wait_send()
            send_chain(p, h, lambda copy: copy.wait_send())
        return carry

    lax.fori_loop(0, 4, settle, 0)


def exchange(residual, attn_partial, norm_gain, router_weight, expert_ids, expert_weight):
    block_rows, width = residual.shape
    wide = width + 128
    units = expert_weight.shape[2]
    vmem = pl.BlockSpec(memory_space=pltpu.VMEM)
    rows_all = 16 * block_rows
    dma = pltpu.SemaphoreType.DMA
    return pl.pallas_call(
        moe_kernel,
        out_shape=jax.ShapeDtypeStruct((block_rows, width), jnp.bfloat16),
        in_specs=[vmem] * 5 + [pl.BlockSpec(memory_space=pl.ANY)],
        out_specs=vmem,
        scratch_shapes=[
            pltpu.VMEM((4, 4 * block_rows, wide), jnp.bfloat16),
            pltpu.VMEM((width, units), jnp.bfloat16),
            pltpu.VMEM((block_rows, width), jnp.float32),
            pltpu.VMEM((block_rows, width), jnp.bfloat16),
            pltpu.VMEM((4, 2, 2, block_rows, width), jnp.bfloat16),
            pltpu.VMEM((4 * block_rows, units), jnp.bfloat16),
            pltpu.VMEM((4, 2, block_rows, width), jnp.bfloat16),
            pltpu.VMEM((4, block_rows, width), jnp.bfloat16),
            pltpu.VMEM((5, block_rows, width), jnp.bfloat16),
            dma, dma((2, 4)), dma((4,)), dma((4, 2)), dma((16,)),
            dma((4,)), dma((4,)), dma((2, 4)), dma((2, 4)), dma((2, 4)), dma((2, 5)),
        ],
        compiler_params=pltpu.CompilerParams(
            collective_id=0, has_side_effects=True, vmem_limit_bytes=56 * 1024 * 1024
        ),
        cost_estimate=pl.CostEstimate(
            flops=4 * rows_all * width * units,
            bytes_accessed=2 * width * units + 16 * block_rows * width,
            transcendentals=rows_all * units,
        ),
    )(residual, attn_partial, norm_gain[None, :], router_weight, expert_ids, expert_weight)


def dense_fits(mesh, row_count, expert_count, top_count):
    return (
        mesh.shape["tensor"] == 1
        and mesh.shape["expert"] == expert_count == 16
        and expert_count <= 4 * top_count
    )


def solution(mesh):
    placed = (
        P(("group", "expert"), "tensor"),
        P("tensor", ("group", "expert"), None),
        P(),
        P("tensor", None),
        P(("group", "expert"), None),
        P("expert", None, "tensor"),
    )

    def run(residual, attn_partial, norm_gain, router_weight, expert_ids, expert_weight):
        dense = dense_fits(mesh, residual.shape[0], router_weight.shape[1], expert_ids.shape[1])
        return jax.shard_map(
            exchange if dense else local,
            mesh=mesh,
            in_specs=placed,
            out_specs=P(("group", "expert"), "tensor"),
            check_vma=False,
        )(residual, attn_partial, norm_gain, router_weight, expert_ids, expert_weight)

    return run
```

```python
import jax
import jax.numpy as jnp
from jax import lax
from jax.experimental import pallas as pl
from jax.experimental.pallas import tpu as pltpu
from jax.sharding import PartitionSpec as P

QBLOCK = 128


EPS = 1e-06
ROUTE_SCALE = 2.5


def encode(values):
    row_count, columns = values.shape
    blocks = values.astype(jnp.float32).reshape(row_count, columns // QBLOCK, QBLOCK)
    largest = jnp.max(jnp.abs(blocks), axis=-1)
    block_scale = ((largest + EPS) / 448.0).astype(jnp.bfloat16)
    encoded = (blocks / block_scale.astype(jnp.float32)[:, :, None]).astype(jnp.bfloat16)
    return (encoded.reshape(row_count, columns), block_scale)


def decode(encoded, block_scale):
    leading = encoded.shape[:-1]
    columns = encoded.shape[-1]
    blocks = encoded.astype(jnp.float32).reshape(leading + (columns // QBLOCK, QBLOCK))
    restored = (blocks * block_scale.astype(jnp.float32)[..., None]).astype(jnp.bfloat16)
    return restored.reshape(leading + (columns,))


def local(residual, attn_partial, norm_gain, router_weight, expert_ids, expert_weight):
    row_count, share_width = residual.shape
    tensor_count = lax.axis_size("tensor")
    model_width = share_width * tensor_count
    expert_count = router_weight.shape[1]
    top_count = expert_ids.shape[1]
    capacity = min(row_count, max(2, 7 * row_count * top_count // (4 * expert_count)))
    first_column = lax.axis_index("tensor") * share_width
    partial_attn = attn_partial[0].astype(jnp.float32)
    full_residual = lax.all_gather(residual, "tensor", axis=1, tiled=True)
    attention = lax.psum(partial_attn.astype(jnp.bfloat16), "tensor").astype(jnp.float32)
    stream = full_residual.astype(jnp.float32) + attention
    meansq = jnp.mean(stream * stream, axis=1, keepdims=True)
    normed = (stream * lax.rsqrt(meansq + EPS) * norm_gain).astype(jnp.bfloat16)
    normed_share = lax.dynamic_slice_in_dim(normed, first_column, share_width, 1)
    stream_share = lax.dynamic_slice_in_dim(stream, first_column, share_width, 1)
    logits = lax.psum(
        jnp.dot(normed_share, router_weight, preferred_element_type=jnp.float32).astype(
            jnp.bfloat16
        ),
        "tensor",
    ).astype(jnp.float32)
    affinity = jax.nn.sigmoid(logits)
    chosen = expert_ids[:, :, None] == jnp.arange(expert_count, dtype=jnp.int32)[None, None, :]
    picked = jnp.sum(jnp.where(chosen, affinity[:, None, :], 0.0), axis=2)
    gate_values = ROUTE_SCALE * picked / jnp.sum(picked, axis=1, keepdims=True)
    encoded, block_scale = encode(normed)
    flat_ids = expert_ids.reshape(-1)
    onehot = (flat_ids[:, None] == jnp.arange(expert_count, dtype=jnp.int32)[None, :]).astype(
        jnp.int32
    )
    before = jnp.cumsum(onehot, axis=0) - onehot
    slot_index = jnp.sum(before * onehot, axis=1)
    target_slot = flat_ids * capacity + slot_index
    source_row = jnp.arange(row_count * top_count, dtype=jnp.int32) // top_count
    send_codes = (
        jnp.zeros((expert_count * capacity, encoded.shape[1]), jnp.bfloat16)
        .at[target_slot]
        .set(encoded[source_row])
    )
    send_scales = (
        jnp.zeros((expert_count * capacity, block_scale.shape[1]), jnp.bfloat16)
        .at[target_slot]
        .set(block_scale[source_row])
    )
    send_codes = send_codes.reshape(expert_count, 1, capacity, encoded.shape[1])
    send_scales = send_scales.reshape(expert_count, 1, capacity, block_scale.shape[1])
    codes_in = lax.all_to_all(send_codes, "expert", split_axis=0, concat_axis=1, tiled=True)
    scales_in = lax.all_to_all(send_scales, "expert", split_axis=0, concat_axis=1, tiled=True)
    inputs = decode(codes_in, scales_in)
    leading = inputs.shape[:-1]
    flat_rows = inputs.reshape(-1, model_width)
    w_expert = expert_weight[0]
    hidden = jax.nn.silu(jnp.dot(flat_rows, w_expert, preferred_element_type=jnp.float32)).astype(
        jnp.bfloat16
    )
    output = lax.dot_general(
        hidden, w_expert, (((1,), (1,)), ((), ())), preferred_element_type=jnp.float32
    ).astype(jnp.bfloat16)
    halves = output.reshape(leading + (tensor_count, 1, share_width))
    returned = lax.all_to_all(
        lax.all_to_all(halves, "expert", split_axis=1, concat_axis=0, tiled=True),
        "tensor",
        split_axis=3,
        concat_axis=4,
        tiled=True,
    )
    expert_out = jnp.sum(returned.astype(jnp.float32), axis=(3, 4)).astype(jnp.bfloat16)
    taken = expert_out.reshape(expert_count * capacity, share_width)[target_slot]
    taken = taken.reshape(row_count, top_count, share_width)
    moe_share = jnp.einsum("rk,rkd->rd", gate_values, taken.astype(jnp.float32))
    return (stream_share + moe_share).astype(jnp.bfloat16)


def moe_kernel(residual_ref, attn_ref, gain_ref, router_ref, ids_ref, weight_hbm, out_ref, rows, weight, stream_ref, stage, share, hidden, core_in, x_in,
               chain_in, weight_sem, line_send, x_send, core_send, row_recv,
               pair_send, pair_recv, half_send, half_recv, chain_send, chain_recv):
    block_rows, width = out_ref.shape
    tile = 256
    me = lax.axis_index("expert")
    z, x, c = me // 4, (me // 2) % 2, me % 2
    flip = z // 2
    m = z + flip * (3 - 2 * z)

    def expert_at(zz, xx, cc):
        return (zz * 2 + xx) * 2 + cc

    def place(o):
        return o + flip * (3 - 2 * o)

    def to(zz, xx, cc):
        return {"expert": expert_at(zz, xx, cc)}

    def slot(zz, xx, cc):
        return rows.at[zz, pl.ds(pl.multiple_of(block_rows * (2 * xx + cc), block_rows), block_rows), :]

    barrier = pltpu.get_barrier_semaphore()

    def greet(device):
        pl.semaphore_signal(barrier, inc=1, device_id=device, device_id_type=pl.DeviceIdType.MESH)

    load_weight = pltpu.make_async_copy(weight_hbm.at[0], weight, weight_sem)
    load_weight.start()
    greet(to(z, 1 - x, c))
    greet(to(z, x, 1 - c))
    pl.when(z > 0)(lambda: greet(to(z - 1, x, c)))
    pl.when(z < 3)(lambda: greet(to(z + 1, x, c)))
    stream = residual_ref[...].astype(jnp.float32) + attn_ref[0].astype(jnp.float32)
    stream_ref[...] = stream
    meansq = jnp.sum(stream * stream, axis=1, keepdims=True) * (1.0 / width)
    inverse = lax.rsqrt(meansq + EPS)
    own = pl.ds(pl.multiple_of(block_rows * (2 * x + c), block_rows), block_rows)
    expert_count = router_ref.shape[1]
    for b in range(width // QBLOCK):
        cols = slice(b * QBLOCK, (b + 1) * QBLOCK)
        normed = (stream_ref[:, cols] * inverse * gain_ref[:, cols]).astype(jnp.bfloat16)
        rows[z, own, cols] = normed
        values = normed.astype(jnp.float32)
        largest = jnp.max(jnp.abs(values), axis=1, keepdims=True)
        scale = ((largest + EPS) / 448.0).astype(jnp.bfloat16).astype(jnp.float32)
        encoded = (values / scale).astype(jnp.bfloat16)
        stage[:, cols] = (encoded.astype(jnp.float32) * scale).astype(jnp.bfloat16)
    logits = jnp.dot(
        rows[z, own, :width], router_ref[...], preferred_element_type=jnp.float32
    )
    rows[z, own, :width] = stage[...]
    affinity = 1.0 / (1.0 + jnp.exp(-logits))
    expert = lax.broadcasted_iota(jnp.int32, logits.shape, 1)
    picked = jnp.zeros_like(affinity)
    for j in range(ids_ref.shape[1]):
        picked += jnp.where(ids_ref[:, j:j + 1] == expert, affinity, 0.0)
    gates = ROUTE_SCALE * picked / jnp.sum(picked, axis=1, keepdims=True)
    high = gates.astype(jnp.bfloat16).astype(jnp.float32)
    spare = jnp.zeros((block_rows, 64 - expert_count), jnp.float32)
    wide_gates = jnp.concatenate([high, spare, gates - high, spare], axis=1)
    rows[z, own, width:] = wide_gates.astype(jnp.bfloat16)
    pl.semaphore_wait(barrier, 3 + m)

    def row_copy(zz, xx, cc, sem, device):
        part = slot(zz, xx, cc)
        return pltpu.make_async_remote_copy(
            src_ref=part, dst_ref=part, send_sem=sem, recv_sem=row_recv.at[expert_at(zz, xx, cc)],
            device_id=device, device_id_type=pl.DeviceIdType.MESH,
        )

    def up_copy(p):
        return row_copy(p, x, c, line_send.at[0, p], to(z + 1, x, c))

    def down_copy(p):
        return row_copy(p, x, c, line_send.at[1, p], to(z - 1, x, c))

    def x_copy(p):
        return row_copy(p, x, c, x_send.at[p], to(z, 1 - x, c))

    def core_copy(p, xx):
        return row_copy(p, xx, c, core_send.at[p, xx], to(z, x, 1 - c))

    def got(zz, xx, cc):
        row_copy(zz, xx, cc, x_send.at[0], to(z, 1 - x, c)).wait_recv()

    def pass_on(p):
        pl.when((p <= z) & (z < 3))(lambda: up_copy(p).start())
        pl.when((p >= z) & (z > 0))(lambda: down_copy(p).start())
        x_copy(p).start()
        core_copy(p, x).start()

    def arrive_line(p):
        got(p, x, c)
        pass_on(p)

    half = width // 256 * 128

    def piece(h):
        return pl.ds(0, half) if h == 0 else pl.ds(half, width - half)

    def pair_copy(p):
        return pltpu.make_async_remote_copy(
            src_ref=share.at[p, 1 - c], dst_ref=core_in.at[p],
            send_sem=pair_send.at[p], recv_sem=pair_recv.at[p],
            device_id=to(z, x, 1 - c), device_id_type=pl.DeviceIdType.MESH,
        )

    def half_copy(p, h):
        return pltpu.make_async_remote_copy(
            src_ref=share.at[p, c, 1 - x, :, piece(h)], dst_ref=x_in.at[p, :, piece(h)],
            send_sem=half_send.at[h, p], recv_sem=half_recv.at[h, p],
            device_id=to(z, 1 - x, c), device_id_type=pl.DeviceIdType.MESH,
        )

    def chain_copy(p, towards, index, h):
        return pltpu.make_async_remote_copy(
            src_ref=share.at[p, c, x, :, piece(h)], dst_ref=chain_in.at[index, :, piece(h)],
            send_sem=chain_send.at[h, p], recv_sem=chain_recv.at[h, index],
            device_id=to(towards, x, c), device_id_type=pl.DeviceIdType.MESH,
        )

    def send_chain(p, h, act):
        pl.when(p > z)(lambda: act(chain_copy(p, z + 1, p, h)))
        pl.when(p == z - 1)(lambda: act(chain_copy(p, z - 1, 4, h)))
        pl.when(p < z - 1)(lambda: act(chain_copy(p, z - 1, p, h)))

    def compute(p):
        units = weight.shape[1]
        gate_block = rows[p, :, width:].astype(jnp.float32)
        lane = lax.broadcasted_iota(jnp.int32, gate_block.shape, 1)
        mine = (lane == me) | (lane == me + 64)
        gate = jnp.sum(jnp.where(mine, gate_block, 0.0), axis=1, keepdims=True)

        def first(n, carry):
            columns = pl.ds(pl.multiple_of(n * tile, tile), tile)
            v = jnp.dot(rows[p, :, :width], weight[:, columns], preferred_element_type=jnp.float32)
            hidden[:, columns] = (v / (1.0 + jnp.exp(-v))).astype(jnp.bfloat16)
            return carry

        lax.fori_loop(0, units // tile, first, 0)

        def second(n, carry):
            columns = pl.ds(pl.multiple_of(n * tile, tile), tile)
            v = lax.dot_general(
                hidden[...], weight[columns, :], (((1,), (1,)), ((), ())),
                preferred_element_type=jnp.float32,
            )
            v = v.astype(jnp.bfloat16).astype(jnp.float32) * gate
            v = v.astype(jnp.bfloat16)
            for i in range(4):
                share[p, i % 2, i // 2, :, columns] = v[i * block_rows:(i + 1) * block_rows]
            return carry

        lax.fori_loop(0, width // tile, second, 0)

    def add_pair(p):
        pair_copy(p).wait_recv()
        share[p, c, 1 - x] = (
            share[p, c, 1 - x].astype(jnp.float32) + core_in[p, 1 - x].astype(jnp.float32)
        ).astype(jnp.bfloat16)
        half_copy(p, 0).start()
        half_copy(p, 1).start()

    def add_half(p, h):
        cols = piece(h)
        half_copy(p, h).wait_recv()
        has = ((p > z) & (z > 0)) | ((p < z) & (z < 3))

        def total():
            return (
                share[p, c, x, :, cols].astype(jnp.float32)
                + core_in[p, x, :, cols].astype(jnp.float32)
                + x_in[p, :, cols].astype(jnp.float32)
            )

        @pl.when(has)
        def _():
            chain_copy(p, z, p, h).wait_recv()
            share[p, c, x, :, cols] = (
                total() + chain_in[p, :, cols].astype(jnp.float32)
            ).astype(jnp.bfloat16)

        @pl.when(jnp.logical_not(has))
        def _():
            share[p, c, x, :, cols] = total().astype(jnp.bfloat16)

        send_chain(p, h, lambda copy: copy.start())

    pass_on(z)
    middle = m == 1

    def step(k, carry):
        own_order = jnp.where(k == 0, m, jnp.where(k == 1, 1 - m, k))
        p = place(own_order)
        later = place(jnp.where(k == 0, 1 - m, k + 1))
        pl.when(k < 3 - 2 * m)(lambda: arrive_line(later))
        pl.when(middle & (k == 0))(lambda: arrive_line(place(2)))
        pl.when(middle & (k == 1))(lambda: arrive_line(place(3)))
        got(p, 1 - x, c)
        core_copy(p, 1 - x).start()
        pl.when(k == 3)(lambda: add_pair(place(2)))
        got(p, x, 1 - c)
        got(p, 1 - x, 1 - c)
        pl.when(k == 0)(lambda: load_weight.wait())
        compute(p)
        pair_copy(p).start()
        return carry

    lax.fori_loop(0, 4, step, 0)

    order = [place(2), place(3), place(1 - m), z]
    add_pair(order[1])
    add_pair(order[2])
    add_half(order[0], 0)
    add_half(order[0], 1)
    add_half(order[1], 0)
    add_half(order[1], 1)
    add_pair(order[3])
    add_half(order[2], 0)
    add_half(order[2], 1)
    for h in range(2):
        cols = piece(h)
        half_copy(z, h).wait_recv()
        stream_ref[:, cols] += (
            share[z, c, x, :, cols].astype(jnp.float32)
            + core_in[z, x, :, cols].astype(jnp.float32)
            + x_in[z, :, cols].astype(jnp.float32)
        )

    for h in range(2):
        cols = piece(h)

        def add_chain(index, cols=cols, h=h):
            chain_copy(z, z, index, h).wait_recv()
            stream_ref[:, cols] += chain_in[index, :, cols].astype(jnp.float32)

        pl.when(z > 0)(lambda f=add_chain: f(z))
        pl.when(z < 3)(lambda f=add_chain: f(4))
        out_ref[:, cols] = stream_ref[:, cols].astype(out_ref.dtype)

    def settle(p, carry):
        pl.when((p <= z) & (z < 3))(lambda: up_copy(p).wait_send())
        pl.when((p >= z) & (z > 0))(lambda: down_copy(p).wait_send())
        x_copy(p).wait_send()
        core_copy(p, 0).wait_send()
        core_copy(p, 1).wait_send()
        pair_copy(p).wait_send()
        for h in range(2):
            half_copy(p, h).wait_send()
            send_chain(p, h, lambda copy: copy.wait_send())
        return carry

    lax.fori_loop(0, 4, settle, 0)


def exchange(residual, attn_partial, norm_gain, router_weight, expert_ids, expert_weight):
    block_rows, width = residual.shape
    wide = width + 128
    units = expert_weight.shape[2]
    vmem = pl.BlockSpec(memory_space=pltpu.VMEM)
    rows_all = 16 * block_rows
    dma = pltpu.SemaphoreType.DMA
    return pl.pallas_call(
        moe_kernel,
        out_shape=jax.ShapeDtypeStruct((block_rows, width), jnp.bfloat16),
        in_specs=[vmem] * 5 + [pl.BlockSpec(memory_space=pl.ANY)],
        out_specs=vmem,
        scratch_shapes=[
            pltpu.VMEM((4, 4 * block_rows, wide), jnp.bfloat16),
            pltpu.VMEM((width, units), jnp.bfloat16),
            pltpu.VMEM((block_rows, width), jnp.float32),
            pltpu.VMEM((block_rows, width), jnp.bfloat16),
            pltpu.VMEM((4, 2, 2, block_rows, width), jnp.bfloat16),
            pltpu.VMEM((4 * block_rows, units), jnp.bfloat16),
            pltpu.VMEM((4, 2, block_rows, width), jnp.bfloat16),
            pltpu.VMEM((4, block_rows, width), jnp.bfloat16),
            pltpu.VMEM((5, block_rows, width), jnp.bfloat16),
            dma, dma((2, 4)), dma((4,)), dma((4, 2)), dma((16,)),
            dma((4,)), dma((4,)), dma((2, 4)), dma((2, 4)), dma((2, 4)), dma((2, 5)),
        ],
        compiler_params=pltpu.CompilerParams(
            collective_id=0, has_side_effects=True, vmem_limit_bytes=56 * 1024 * 1024
        ),
        cost_estimate=pl.CostEstimate(
            flops=4 * rows_all * width * units,
            bytes_accessed=2 * width * units + 16 * block_rows * width,
            transcendentals=rows_all * units,
        ),
    )(residual, attn_partial, norm_gain[None, :], router_weight, expert_ids, expert_weight)


def dense_fits(mesh, row_count, expert_count, top_count):
    return (
        mesh.shape["tensor"] == 1
        and mesh.shape["expert"] == expert_count == 16
        and expert_count <= 4 * top_count
    )


def solution(mesh):
    placed = (
        P(("group", "expert"), "tensor"),
        P("tensor", ("group", "expert"), None),
        P(),
        P("tensor", None),
        P(("group", "expert"), None),
        P("expert", None, "tensor"),
    )

    def run(residual, attn_partial, norm_gain, router_weight, expert_ids, expert_weight):
        dense = dense_fits(mesh, residual.shape[0], router_weight.shape[1], expert_ids.shape[1])
        return jax.shard_map(
            exchange if dense else local,
            mesh=mesh,
            in_specs=placed,
            out_specs=P(("group", "expert"), "tensor"),
            check_vma=False,
        )(residual, attn_partial, norm_gain, router_weight, expert_ids, expert_weight)

    return run
```
